32 devices in a mesh: grp: 2 (over y), seq: 4 (over z), head: 2 (over x), rep: 2 (over core).
Axes of the slice: x: 2, y: 2, z: 4, core: 2. Of those that a mesh axis runs over, the one named last changes fastest.
Arguments:
- latents: bfloat16 [2048, 1024], P(('grp', 'seq', 'rep')), parts along dimension 0, may hold values from -6 to 6
- cotangent: bfloat16 [2048, 1024], P(('grp', 'seq', 'rep')), parts along dimension 0, may hold values from -12 to 12
- tokens: bfloat16 [4096, 1024], P(('grp', 'seq', 'rep')), parts along dimension 0, may hold values from -200 to 200
- counts: int32 [16], P(('grp', 'seq', 'rep')), parts along dimension 0, may hold values from 1 to 256, 1280 in all
- w_query: bfloat16 [1024, 1024], P(None, 'head'), may hold values from -0.1875 to 0.1875
- w_key: bfloat16 [1024, 1024], P(None, 'head'), may hold values from -0.1875 to 0.1875
- w_value: bfloat16 [1024, 1024], P(None, 'head'), may hold values from -0.1875 to 0.1875
- w_out: bfloat16 [1024, 1024], P('head'), may hold values from -0.1875 to 0.1875
Outputs:
- attended: bfloat16 [2048, 1024], P(('grp', 'seq', 'rep'), 'head'), parts along dimension 0
- latent_grad: bfloat16 [2048, 1024], P(('grp', 'seq', 'rep'), 'head'), parts along dimension 0
- token_grad: bfloat16 [4096, 1024], P(('grp', 'seq', 'rep'), 'head'), parts along dimension 0
The draws below stay inside these ranges and needn't reach their ends.
There are 2 independent parts, one for each index of `grp`. The reference program is written for one: setup_inputs(seed, part) draws one part's arguments, and reference() takes and returns one part's arrays. A program takes and returns all parts, laid end to end along the dimension named above; an argument that names none is the same for every part. Nothing has to cross between parts.
Inputs may be any that keep to these rules, and one draw needn't show every extreme that they name: The counts of a group sum to 1280; the largest equals 256.
All inputs are finite; a program needn't handle non-finite values.
Results may differ from the reference program's by a relative error of at most 0.039.
The reference program's roundings to bfloat16 on the way count: a program that leaves them out, or rounds other values in their place, can miss the bound.
Values may be sent and summed in bfloat16 or wider, within the bound.
A program may use at most 128 MiB of HBM per device.

```python
import math
import jax
import jax.numpy as jnp
import numpy as np
from jax import lax

D = 1024
LAT = 1024
HEADS = 16
TOK_DEV = 256
TOKENS = 2048
N_SEQ = 4
N_HEAD = 2
N_REP = 2


def draw_tokens(key, part):
    seed_base = jax.random.fold_in(key, 0)
    result = jnp.clip(2.5 * jax.random.normal(seed_base, (TOKENS, D), jnp.float32), -15.0, 15.0)
    return result.astype(jnp.bfloat16)


def steps_of(rng, extent, cuts, low, high):
    loudness, own = 1.0, jax.random.fold_in(rng, 6)
    for dim, parts in cuts:
        draws = jnp.exp(jax.random.uniform(jax.random.fold_in(own, dim), (parts,), jnp.float32, low / len(cuts), high / len(cuts)))
        loudness = loudness * jnp.repeat(draws, extent[dim] // parts).reshape([-1 if axis == dim else 1 for axis in range(len(extent))])
    return loudness


def length_profile(number_of, total, limit, skew):
    portions = [(1 << 20) // math.isqrt(grade ** skew) + 1 for grade in range(2, number_of + 1)]
    spare, holding = total - limit - (number_of - 1), [1] * (number_of - 1)
    while spare > 0:
        candidates = [i for i in range(number_of - 1) if holding[i] < limit]
        whole, remaining = sum([portions[i] for i in candidates]), spare
        for i in candidates:
            addition = min(limit - holding[i], max(1, remaining * portions[i] // whole), spare)
            holding[i] = holding[i] + addition
            spare = spare - addition
    return np.array([limit] + holding)


def ragged(own_key, amount, total, reach, slope):
    if amount == 2:
        one = jax.random.randint(own_key, (), max(1, total - reach), min(reach, total - 1) + 1)
        return jnp.stack([one, total - one])
    sizes = jnp.asarray(length_profile(amount, total, reach, slope), jnp.int32)
    twos = (amount - 1) // 2
    source_of, sink = sizes[1:1 + 2 * twos:2], sizes[2:2 + 2 * twos:2]
    slack = jnp.minimum(source_of - 1, reach - sink)
    passed = jax.random.randint(jax.random.fold_in(own_key, 1), (twos,), 0, 1 << 20) % (slack + 1)
    sizes = sizes.at[1:1 + 2 * twos:2].set(source_of - passed).at[2:2 + 2 * twos:2].set(sink + passed)
    return sizes[jax.random.permutation(jax.random.fold_in(own_key, 2), amount)]


def noise(stream_key, dims, scale, most, cuts=(), held_as=jnp.bfloat16):
    array = jax.random.normal(stream_key, dims, jnp.float32) * scale
    if len(cuts) > 0:
        array = steps_of(stream_key, dims, cuts, -0.22, 0.18) * array
    return jnp.clip(array, min=-most, max=most).astype(held_as)


def setup_inputs(seed: int = 0, part: int = 0) -> dict:
    key_list = jax.random.split(jax.random.key(seed), 9)
    part_keys = jax.random.split(jax.random.fold_in(key_list[8], part), 9)
    return {
        "latents": noise(part_keys[0], (LAT, D), 1.0, 6.0, ((0, 8),)),
        "cotangent": noise(part_keys[1], (LAT, D), 2.0, 12.0, ((0, 8),)),
        "tokens": draw_tokens(jax.random.fold_in(jax.random.fold_in(key_list[8], part), 71), part),
        "counts": ragged(part_keys[3], N_SEQ * N_REP, TOKENS * 5 // 8, TOK_DEV, 2).astype(jnp.int32),
        "w_query": noise(key_list[4], (D, D), D ** -0.5, 0.1875, ((1, 2),)),
        "w_key": noise(key_list[5], (D, D), D ** -0.5, 0.1875, ((1, 2),)),
        "w_value": noise(key_list[6], (D, D), D ** -0.5, 0.1875, ((1, 2),)),
        "w_out": noise(key_list[7], (D, D), D ** -0.5, 0.1875, ((0, 2),)),
    }


def rounded(matrix):
    return lax.optimization_barrier(matrix.astype(jnp.bfloat16)).astype(jnp.float32)


def reference(latents, cotangent, tokens, counts, w_query, w_key, w_value, w_out):
    shard_count = N_SEQ * N_REP
    head_size = D // HEADS
    group_width = D // N_HEAD
    scale = head_size ** -0.5
    queries = jnp.dot(latents, w_query, preferred_element_type=jnp.float32).astype(jnp.bfloat16)
    grad_att = jnp.dot(cotangent, w_out.T, preferred_element_type=jnp.float32).astype(jnp.bfloat16)
    key_rows = jnp.dot(tokens, w_key, preferred_element_type=jnp.float32).astype(jnp.bfloat16)
    value_rows = jnp.dot(tokens, w_value, preferred_element_type=jnp.float32).astype(jnp.bfloat16)
    query_heads = queries.astype(jnp.float32).reshape(LAT, HEADS, head_size).transpose(1, 0, 2)
    grad_heads = grad_att.astype(jnp.float32).reshape(LAT, HEADS, head_size).transpose(1, 0, 2)
    key_shards = key_rows.astype(jnp.float32).reshape(shard_count, TOK_DEV, HEADS, head_size)
    value_shards = value_rows.astype(jnp.float32).reshape(shard_count, TOK_DEV, HEADS, head_size)
    positions = jnp.arange(TOK_DEV, dtype=jnp.int32)

    def masked_scores(key_part, live_count):
        scores = jnp.einsum("hld,thd->hlt", query_heads, key_part) * scale
        return jnp.where((positions < live_count)[None, None, :], scores, -jnp.inf)

    def forward_part(shard_item):
        key_part, value_part, live_count = shard_item
        scores = masked_scores(key_part, live_count)
        highest = jnp.max(scores, axis=2)
        expo = jnp.exp(scores - highest[:, :, None])
        totals = jnp.sum(expo, axis=2)
        weighted = jnp.einsum("hlt,thd->hld", rounded(expo), value_part)
        return highest, totals, weighted

    highs, totals, weighted = lax.map(forward_part, (key_shards, value_shards, counts))
    peak = jnp.max(highs, axis=0)
    factor = jnp.exp(highs - peak[None])
    denominator = jnp.sum(totals * factor, axis=0)
    attention = jnp.sum(weighted * factor[..., None], axis=0) / denominator[..., None]
    log_norms = peak + jnp.log(denominator)
    attention_b = attention.transpose(1, 0, 2).reshape(LAT, D).astype(jnp.bfloat16)

    attended = jnp.zeros((LAT, D), jnp.float32)
    for group_index in range(N_HEAD):
        lower = group_index * group_width
        part_term = jnp.dot(attention_b[:, lower:lower + group_width], w_out[lower:lower + group_width, :], preferred_element_type=jnp.float32)
        attended = attended + rounded(part_term)
    attended = attended.astype(jnp.bfloat16)

    row_terms = jnp.sum((attention_b.astype(jnp.float32) * grad_att.astype(jnp.float32)).reshape(LAT, HEADS, head_size), axis=2).T

    def backward_part(shard_item):
        key_part, value_part, live_count = shard_item
        scores = masked_scores(key_part, live_count)
        weights = jnp.exp(scores - log_norms[:, :, None])
        grad_value = jnp.einsum("hlt,hld->thd", rounded(weights), grad_heads).astype(jnp.bfloat16)
        grad_weights = jnp.einsum("hld,thd->hlt", grad_heads, value_part)
        grad_scores = rounded(weights * (grad_weights - row_terms[:, :, None]) * scale)
        query_terms = jnp.einsum("hlt,thd->hld", grad_scores, key_part)
        grad_key = jnp.einsum("hlt,hld->thd", grad_scores, query_heads).astype(jnp.bfloat16)
        return query_terms, grad_key, grad_value

    query_terms, grad_keys, grad_values = lax.map(backward_part, (key_shards, value_shards, counts))
    query_grad = jnp.sum(query_terms, axis=0).transpose(1, 0, 2).reshape(LAT, D).astype(jnp.bfloat16)
    latent_grad = jnp.dot(query_grad, w_query.T, preferred_element_type=jnp.float32).astype(jnp.bfloat16)

    grad_key_all = grad_keys.reshape(TOKENS, D)
    grad_value_all = grad_values.reshape(TOKENS, D)
    token_grad = jnp.zeros((TOKENS, D), jnp.float32)
    for group_index in range(N_HEAD):
        lower = group_index * group_width
        upper = lower + group_width
        part_term = jnp.dot(grad_key_all[:, lower:upper], w_key[:, lower:upper].T, preferred_element_type=jnp.float32)
        part_term = part_term + jnp.dot(grad_value_all[:, lower:upper], w_value[:, lower:upper].T, preferred_element_type=jnp.float32)
        token_grad = token_grad + rounded(part_term)
    token_grad = token_grad.astype(jnp.bfloat16)
    return attended, latent_grad, token_grad
```

```python
import functools

import jax
import jax.numpy as jnp
from jax import lax
from jax.experimental import pallas as pl
from jax.experimental.pallas import tpu as pltpu
from jax.sharding import PartitionSpec as P

D = 1024
HEADS = 16


def combined_all(value, axis, join):
    pieces = jax.tree.map(lambda part: lax.all_gather(part, axis), value)
    head = jax.tree.map(lambda part: part[0], pieces)
    tail = jax.tree.map(lambda part: part[1:], pieces)
    running, _ = lax.scan(lambda running, slab: (join(running, slab), None), head, tail)
    return running


def merge_parts(earlier, latter):
    high_first, sums_first, accum_first = earlier
    high_second, sums_second, accum_second = latter
    highest = jnp.maximum(high_first, high_second)
    factor_first = jnp.exp(high_first - highest)
    factor_second = jnp.exp(high_second - highest)
    repeats = accum_first.shape[-1] // high_first.shape[-1]
    merged = accum_first * jnp.repeat(factor_first, repeats, axis=-1) + accum_second * jnp.repeat(
        factor_second, repeats, axis=-1
    )
    return (highest, sums_first * factor_first + sums_second * factor_second, merged)


def head_major(matrix, heads_here):
    rows_count = matrix.shape[0]
    return matrix.reshape(rows_count, heads_here, matrix.shape[1] // heads_here).transpose(1, 0, 2)


def row_major(stacked):
    return stacked.transpose(1, 0, 2).reshape(stacked.shape[1], stacked.shape[0] * stacked.shape[2])


def contract_last(left, right):
    return lax.dot_general(
        left, right, (((1,), (1,)), ((), ())), preferred_element_type=jnp.float32
    )


def contract_first(left, right):
    return lax.dot_general(
        left, right, (((0,), (0,)), ((), ())), preferred_element_type=jnp.float32
    )


def on_device(latents, cotangent, tokens, counts, w_query, w_key, w_value, w_out):
    columns = w_query.shape[1]
    head_size = D // HEADS
    heads_here = columns // head_size
    scale = head_size ** (-0.5)
    lat_rows = latents.shape[0]
    row_start = lax.axis_index(("seq", "rep")) * lat_rows
    query_rows = jnp.dot(latents, w_query, preferred_element_type=jnp.float32).astype(jnp.bfloat16)
    grad_rows = contract_last(cotangent, w_out).astype(jnp.bfloat16)
    queries, grad_att = (
        lax.all_gather(query_rows, ("seq", "rep"), axis=0, tiled=True),
        lax.all_gather(grad_rows, ("seq", "rep"), axis=0, tiled=True),
    )
    key_rows = jnp.dot(tokens, w_key, preferred_element_type=jnp.float32).astype(jnp.bfloat16)
    value_rows = jnp.dot(tokens, w_value, preferred_element_type=jnp.float32).astype(jnp.bfloat16)
    live_mask = jnp.arange(tokens.shape[0], dtype=jnp.int32) < counts[0]
    query_heads = head_major(queries, heads_here)
    grad_heads = head_major(grad_att, heads_here)
    key_heads = head_major(key_rows, heads_here)
    value_heads = head_major(value_rows, heads_here)

    def masked_scores(query_head, key_head):
        scores = contract_last(query_head, key_head) * scale
        return jnp.where(live_mask[None, :], scores, -jnp.inf)

    def forward_head(operands):
        query_head, key_head, value_head = operands
        scores = masked_scores(query_head, key_head)
        highest = jnp.max(scores, axis=1)
        expo = jnp.exp(scores - highest[:, None])
        weighted = jnp.dot(
            expo.astype(jnp.bfloat16), value_head, preferred_element_type=jnp.float32
        )
        return (highest, jnp.sum(expo, axis=1), weighted)

    highs, sums, accums = lax.map(forward_head, (query_heads, key_heads, value_heads))
    highs = highs.T
    sums = sums.T
    accums = row_major(accums)
    highest, denominator, numerator = combined_all(
        (highs, sums, accums), ("seq", "rep"), merge_parts
    )
    attention = (numerator / jnp.repeat(denominator, head_size, axis=1)).astype(jnp.bfloat16)
    log_norms = highest + jnp.log(denominator)
    all_rows = attention.shape[0]
    row_terms = jnp.sum(
        (attention.astype(jnp.float32) * grad_att.astype(jnp.float32)).reshape(
            all_rows, heads_here, head_size
        ),
        axis=2,
    )
    attended_rows = lax.dynamic_slice_in_dim(attention, row_start, lat_rows, 0)
    out_terms = jnp.dot(attended_rows, w_out, preferred_element_type=jnp.float32)
    attended = lax.psum_scatter(
        out_terms.astype(jnp.bfloat16), "head", scatter_dimension=1, tiled=True
    )

    def backward_head(operands):
        query_head, key_head, value_head, grad_head, log_norm, row_term = operands
        scores = masked_scores(query_head, key_head)
        weights = jnp.exp(scores - log_norm[:, None])
        grad_value = contract_first(weights.astype(jnp.bfloat16), grad_head).astype(jnp.bfloat16)
        grad_weights = contract_last(grad_head, value_head)
        grad_scores = (weights * (grad_weights - row_term[:, None]) * scale).astype(jnp.bfloat16)
        query_term = jnp.dot(grad_scores, key_head, preferred_element_type=jnp.float32)
        grad_key = contract_first(grad_scores, query_head).astype(jnp.bfloat16)
        return (query_term, grad_key, grad_value)

    query_terms, grad_keys, grad_values = lax.map(
        backward_head, (query_heads, key_heads, value_heads, grad_heads, log_norms.T, row_terms.T)
    )
    query_terms = row_major(query_terms)
    query_total = lax.psum(query_terms, ("seq", "rep"))
    query_grad = lax.dynamic_slice_in_dim(query_total, row_start, lat_rows, 0)
    latent_terms = contract_last(query_grad.astype(jnp.bfloat16), w_query)
    latent_grad = lax.psum_scatter(latent_terms, "head", scatter_dimension=1, tiled=True).astype(
        jnp.bfloat16
    )
    token_terms = contract_last(row_major(grad_keys), w_key) + contract_last(
        row_major(grad_values), w_value
    )
    token_grad = lax.psum_scatter(
        token_terms.astype(jnp.bfloat16), "head", scatter_dimension=1, tiled=True
    )
    return (attended, latent_grad, token_grad)


MESH = pl.DeviceIdType.MESH
BF = jnp.bfloat16
F32 = jnp.float32


def remote(src, dst, send, recv, device):
    return pltpu.make_async_remote_copy(
        src_ref=src, dst_ref=dst, send_sem=send, recv_sem=recv, device_id=device, device_id_type=MESH
    )


def fused_kernel(
    n_seq, n_head, n_rep,
    latents, cotangent, tokens, counts, w_query, w_key, w_value, w_out,
    attended, latent_grad, token_grad,
    q_all, g_all, g_t, k_all, v_all, k_t, v_t, bias, expo, highs,
    acc_send, acc_recv, st_send, st_recv, norm_row, dq_send, dq_recv, dk, dv, dkv_send, dkv_recv,
    att_stage, att_recv, lat_stage, lat_recv, tok_stage, tok_recv,
    z_send, z_recv, r_send, r_recv, h_send, h_recv,
):
    lat, tok, cols = latents.shape[0], tokens.shape[0], w_query.shape[1]
    hd = D // HEADS
    wide = 2 * hd
    pairs = cols // wide
    scale = hd ** (-0.5)
    z, h, r = lax.axis_index("seq"), lax.axis_index("head"), lax.axis_index("rep")
    other = 1 - r

    def zp(k):
        return lax.rem(z + k, n_seq)

    def hp(k):
        return lax.rem(h + k, n_head)

    barrier = pltpu.get_barrier_semaphore()
    for k in range(1, n_seq):
        pl.semaphore_signal(barrier, inc=1, device_id={"seq": zp(k)}, device_id_type=MESH)
    for k in range(1, n_head):
        pl.semaphore_signal(barrier, inc=1, device_id={"head": hp(k)}, device_id_type=MESH)
    pl.semaphore_signal(barrier, inc=1, device_id={"rep": other}, device_id_type=MESH)

    def z_copy(kind, src, dst, peer, slot_send, slot_recv):
        return remote(src, dst, z_send.at[kind, slot_send], z_recv.at[kind, slot_recv], {"seq": peer})

    def q_copy(peer, owner):
        return z_copy(0, q_all.at[owner], q_all.at[owner], peer, peer, owner)

    def g_copy(peer, owner):
        return z_copy(1, g_all.at[owner], g_all.at[owner], peer, peer, owner)

    def acc_copy(peer, sender):
        return z_copy(2, acc_send.at[peer], acc_recv.at[sender], peer, peer, sender)

    def st_copy(peer, sender):
        return z_copy(3, st_send.at[peer], st_recv.at[sender], peer, peer, sender)

    def norm_copy(peer, owner):
        return z_copy(4, norm_row.at[owner], norm_row.at[owner], peer, peer, owner)

    def dq_copy(peer, sender):
        return z_copy(5, dq_send.at[peer], dq_recv.at[sender], peer, peer, sender)

    def r_copy(index, src, dst):
        return remote(src, dst, r_send.at[index], r_recv.at[index], {"rep": other})

    own, theirs = pl.ds(0, tok), pl.ds(tok, tok)
    k_copy = r_copy(0, k_all.at[own], k_all.at[theirs])
    v_copy = r_copy(1, v_all.at[own], v_all.at[theirs])
    b_copy = r_copy(2, bias.at[own], bias.at[theirs])
    dkv_copy = r_copy(3, dkv_send, dkv_recv)

    def h_copy(index, stage, landing, peer, sender):
        return remote(
            stage.at[peer], landing.at[sender], h_send.at[index, peer], h_recv.at[index, sender], {"head": peer}
        )

    q_all[z] = (jnp.dot(latents[...], w_query[...], preferred_element_type=F32).astype(BF) * scale).astype(BF)
    pl.semaphore_wait(barrier, n_seq - 1 + n_head - 1 + 1)
    for k in range(1, n_seq):
        q_copy(zp(k), z).start()
    k_all[own, :] = jnp.dot(tokens[...], w_key[...], preferred_element_type=F32).astype(BF)
    k_copy.start()
    rows = lax.broadcasted_iota(jnp.int32, (tok, 128), 0)
    bias[own, :] = jnp.where(rows < counts[0], 0.0, -jnp.inf).astype(F32)
    b_copy.start()
    v_all[own, :] = jnp.dot(tokens[...], w_value[...], preferred_element_type=F32).astype(BF)
    v_copy.start()
    grads = contract_last(cotangent[...], w_out[...])
    g_all[z] = grads.astype(BF)
    for k in range(1, n_seq):
        g_copy(zp(k), z).start()
    g_t[...] = grads.T.astype(BF)
    k_t[:, 0:tok] = k_all[own, :].astype(F32).T.astype(BF)
    v_t[:, 0:tok] = v_all[own, :].astype(F32).T.astype(BF)
    k_copy.wait_recv()
    k_t[:, tok:2 * tok] = k_all[theirs, :].astype(F32).T.astype(BF)
    b_copy.wait_recv()
    v_copy.wait_recv()
    v_t[:, tok:2 * tok] = v_all[theirs, :].astype(F32).T.astype(BF)

    lane = lax.broadcasted_iota(jnp.int32, (lat, wide), 1)
    upper = lax.broadcasted_iota(jnp.int32, (wide, lat), 0)

    def stacked(block):
        zero = jnp.zeros_like(block)
        return jnp.concatenate([jnp.where(lane < hd, block, zero), jnp.where(lane < hd, zero, block)], axis=0)

    def halves(both):
        return jnp.where(upper < hd, both[:, :lat], both[:, lat:])

    def forward(j, acc_out, stat_out):
        for p in range(pairs):
            span = slice(p * wide, (p + 1) * wide)
            qs = stacked(q_all[j, :, span])
            live = bias[...]
            scores = contract_last(k_all[:, span], qs)
            scores = scores + jnp.concatenate([live] * (2 * lat // 128), axis=1)
            high = jnp.max(scores, axis=0, keepdims=True)
            e = jnp.exp(scores - high)
            expo[j, p] = e
            highs[j, p] = high
            stat_out[p, 0:1, :] = high
            stat_out[p, 1:2, :] = jnp.sum(e, axis=0, keepdims=True)
            out = jnp.dot(v_t[span, :], e.astype(BF), preferred_element_type=F32)
            acc_out[span, :] = halves(out).astype(BF)

    forward(z, acc_recv.at[z], st_recv.at[z])

    def forward_step(k, carry):
        j = zp(k)
        q_copy(j, j).wait_recv()
        forward(j, acc_send.at[j], st_send.at[j])
        acc_copy(j, z).start()
        st_copy(j, z).start()
        return carry

    lax.fori_loop(1, n_seq, forward_step, 0)

    for k in range(1, n_seq):
        acc_copy(zp(k), zp(k)).wait_recv()
        st_copy(zp(k), zp(k)).wait_recv()

    att_rows = []
    for p in range(pairs):
        span = slice(p * wide, (p + 1) * wide)
        highest = st_recv[0, p, 0:1, :]
        for s in range(1, n_seq):
            highest = jnp.maximum(highest, st_recv[s, p, 0:1, :])
        total = jnp.zeros_like(highest)
        numerator = jnp.zeros((wide, lat), F32)
        for s in range(n_seq):
            factor = jnp.exp(st_recv[s, p, 0:1, :] - highest)
            total = total + st_recv[s, p, 1:2, :] * factor
            spread = jnp.where(upper < hd, factor[:, :lat], factor[:, lat:])
            numerator = numerator + acc_recv[s, span, :].astype(F32) * spread
        below = jnp.where(upper < hd, total[:, :lat], total[:, lat:])
        att = (numerator / below).astype(BF).astype(F32)
        att_rows.append(att)
        product = att * g_t[span, :].astype(F32)
        norm_row[z, p, 0:1, :] = highest + jnp.log(total)
        norm_row[z, p, 1:2, :] = jnp.concatenate(
            [jnp.sum(product[:hd], axis=0, keepdims=True), jnp.sum(product[hd:], axis=0, keepdims=True)], axis=1
        )
    for k in range(1, n_seq):
        norm_copy(zp(k), z).start()

    def stage_columns(stage, terms):
        for g in range(n_head):
            stage[g] = terms[:, g * cols:(g + 1) * cols].astype(BF)

    attention = jnp.concatenate([part.T for part in att_rows], axis=1).astype(BF)
    stage_columns(att_stage, jnp.dot(attention, w_out[...], preferred_element_type=F32))
    for k in range(1, n_head):
        h_copy(0, att_stage, att_recv, hp(k), h).start()

    dk[...] = jnp.zeros_like(dk)
    dv[...] = jnp.zeros_like(dv)

    def backward(j, dq_out):
        for p in range(pairs):
            span = slice(p * wide, (p + 1) * wide)
            qs = stacked(q_all[j, :, span])
            gs = stacked(g_all[j, :, span])
            weights = expo[j, p] * jnp.exp(highs[j, p] - norm_row[j, p, 0:1, :])
            dv[:, span] += jnp.dot(weights.astype(BF), gs, preferred_element_type=F32)
            inner = contract_last(v_all[:, span], gs)
            ds = (weights * (inner - norm_row[j, p, 1:2, :])).astype(BF)
            dk[:, span] += jnp.dot(ds, qs, preferred_element_type=F32)
            both = jnp.dot(k_t[span, :], ds, preferred_element_type=F32)
            dq_out[span, :] = (halves(both) * scale).astype(BF)

    backward(z, dq_recv.at[z])

    def backward_step(k, carry):
        j = zp(k)
        g_copy(j, j).wait_recv()
        norm_copy(j, j).wait_recv()
        backward(j, dq_send.at[j])
        dq_copy(j, z).start()
        return carry

    lax.fori_loop(1, n_seq, backward_step, 0)

    dkv_send[0] = dk[theirs, :].astype(BF)
    dkv_send[1] = dv[theirs, :].astype(BF)
    dkv_copy.start()

    dkv_copy.wait_recv()
    grad_key = (dk[own, :] + dkv_recv[0].astype(F32)).astype(BF)
    grad_value = (dv[own, :] + dkv_recv[1].astype(F32)).astype(BF)
    stage_columns(tok_stage, contract_last(grad_key, w_key[...]) + contract_last(grad_value, w_value[...]))
    for k in range(1, n_head):
        h_copy(1, tok_stage, tok_recv, hp(k), h).start()

    for k in range(1, n_seq):
        dq_copy(zp(k), zp(k)).wait_recv()
    total_t = dq_recv[0].astype(F32)
    for s in range(1, n_seq):
        total_t = total_t + dq_recv[s].astype(F32)
    stage_columns(lat_stage, contract_last(total_t.T.astype(BF), w_query[...]))
    for k in range(1, n_head):
        h_copy(2, lat_stage, lat_recv, hp(k), h).start()

    def summed(index, stage, landing, out):
        total = stage[h].astype(F32)
        for k in range(1, n_head):
            h_copy(index, stage, landing, hp(k), hp(k)).wait_recv()
            total = total + landing[hp(k)].astype(F32)
        out[...] = total.astype(BF)

    summed(0, att_stage, att_recv, attended)
    summed(1, tok_stage, tok_recv, token_grad)
    summed(2, lat_stage, lat_recv, latent_grad)

    for k in range(1, n_seq):
        peer = zp(k)
        for make in (q_copy, g_copy, acc_copy, st_copy, norm_copy, dq_copy):
            make(peer, z).wait_send()
    for copy in (k_copy, v_copy, b_copy, dkv_copy):
        copy.wait_send()
    for k in range(1, n_head):
        h_copy(0, att_stage, att_recv, hp(k), h).wait_send()
        h_copy(1, tok_stage, tok_recv, hp(k), h).wait_send()
        h_copy(2, lat_stage, lat_recv, hp(k), h).wait_send()


def fused(n_seq, n_head, n_rep, latents, cotangent, tokens, counts, w_query, w_key, w_value, w_out):
    lat, tok, cols = latents.shape[0], tokens.shape[0], w_query.shape[1]
    wide = 2 * D // HEADS
    pairs = cols // wide
    vmem = pltpu.VMEM
    dma = pltpu.SemaphoreType.DMA
    stats = vmem((n_seq, pairs, 2, 2 * lat), F32)
    block = vmem((n_seq, cols, lat), BF)
    scratch = [
        vmem((n_seq, lat, cols), BF),
        vmem((n_seq, lat, cols), BF),
        vmem((cols, lat), BF),
        vmem((2 * tok, cols), BF),
        vmem((2 * tok, cols), BF),
        vmem((cols, 2 * tok), BF),
        vmem((cols, 2 * tok), BF),
        vmem((2 * tok, 128), F32),
        vmem((n_seq, pairs, 2 * tok, 2 * lat), F32),
        vmem((n_seq, pairs, 1, 2 * lat), F32),
        block,
        block,
        stats,
        stats,
        stats,
        block,
        block,
        vmem((2 * tok, cols), F32),
        vmem((2 * tok, cols), F32),
        vmem((2, tok, cols), BF),
        vmem((2, tok, cols), BF),
        vmem((n_head, lat, cols), BF),
        vmem((n_head, lat, cols), BF),
        vmem((n_head, lat, cols), BF),
        vmem((n_head, lat, cols), BF),
        vmem((n_head, tok, cols), BF),
        vmem((n_head, tok, cols), BF),
        dma((6, n_seq)),
        dma((6, n_seq)),
        dma((4,)),
        dma((4,)),
        dma((3, n_head)),
        dma((3, n_head)),
    ]
    whole = pl.BlockSpec(memory_space=pltpu.VMEM)
    return pl.pallas_call(
        functools.partial(fused_kernel, n_seq, n_head, n_rep),
        out_shape=(
            jax.ShapeDtypeStruct((lat, cols), BF),
            jax.ShapeDtypeStruct((lat, cols), BF),
            jax.ShapeDtypeStruct((tok, cols), BF),
        ),
        in_specs=[whole] * 3 + [pl.BlockSpec(memory_space=pltpu.SMEM)] + [whole] * 4,
        out_specs=(whole,) * 3,
        scratch_shapes=scratch,
        compiler_params=pltpu.CompilerParams(
            collective_id=0, has_side_effects=True, vmem_limit_bytes=48 * 1024 * 1024
        ),
    )(latents, cotangent, tokens, counts, w_query, w_key, w_value, w_out)


def solution(mesh):
    in_specs = (
        P(("grp", "seq", "rep"), None),
        P(("grp", "seq", "rep"), None),
        P(("grp", "seq", "rep"), None),
        P(("grp", "seq", "rep")),
        P(None, "head"),
        P(None, "head"),
        P(None, "head"),
        P("head", None),
    )
    out_specs = (
        P(("grp", "seq", "rep"), "head"),
        P(("grp", "seq", "rep"), "head"),
        P(("grp", "seq", "rep"), "head"),
    )
    n_seq, n_head, n_rep = mesh.shape["seq"], mesh.shape["head"], mesh.shape["rep"]

    def body(*operands):
        if operands[0].shape[0] % 128 == 0 and n_rep == 2:
            return fused(n_seq, n_head, n_rep, *operands)
        return on_device(*operands)

    return jax.shard_map(
        body, mesh=mesh, in_specs=in_specs, out_specs=out_specs, check_vma=False
    )
```

```python
import functools

import jax
import jax.numpy as jnp
from jax import lax
from jax.experimental import pallas as pl
from jax.experimental.pallas import tpu as pltpu
from jax.sharding import PartitionSpec as P

D = 1024
HEADS = 16


def combined_all(value, axis, join):
    pieces = jax.tree.map(lambda part: lax.all_gather(part, axis), value)
    head = jax.tree.map(lambda part: part[0], pieces)
    tail = jax.tree.map(lambda part: part[1:], pieces)
    running, _ = lax.scan(lambda running, slab: (join(running, slab), None), head, tail)
    return running


def merge_parts(earlier, latter):
    high_first, sums_first, accum_first = earlier
    high_second, sums_second, accum_second = latter
    highest = jnp.maximum(high_first, high_second)
    factor_first = jnp.exp(high_first - highest)
    factor_second = jnp.exp(high_second - highest)
    repeats = accum_first.shape[-1] // high_first.shape[-1]
    merged = accum_first * jnp.repeat(factor_first, repeats, axis=-1) + accum_second * jnp.repeat(
        factor_second, repeats, axis=-1
    )
    return (highest, sums_first * factor_first + sums_second * factor_second, merged)


def head_major(matrix, heads_here):
    rows_count = matrix.shape[0]
    return matrix.reshape(rows_count, heads_here, matrix.shape[1] // heads_here).transpose(1, 0, 2)


def row_major(stacked):
    return stacked.transpose(1, 0, 2).reshape(stacked.shape[1], stacked.shape[0] * stacked.shape[2])


def contract_last(left, right):
    return lax.dot_general(
        left, right, (((1,), (1,)), ((), ())), preferred_element_type=jnp.float32
    )


def contract_first(left, right):
    return lax.dot_general(
        left, right, (((0,), (0,)), ((), ())), preferred_element_type=jnp.float32
    )


def on_device(latents, cotangent, tokens, counts, w_query, w_key, w_value, w_out):
    columns = w_query.shape[1]
    head_size = D // HEADS
    heads_here = columns // head_size
    scale = head_size ** (-0.5)
    lat_rows = latents.shape[0]
    row_start = lax.axis_index(("seq", "rep")) * lat_rows
    query_rows = jnp.dot(latents, w_query, preferred_element_type=jnp.float32).astype(jnp.bfloat16)
    grad_rows = contract_last(cotangent, w_out).astype(jnp.bfloat16)
    queries, grad_att = (
        lax.all_gather(query_rows, ("seq", "rep"), axis=0, tiled=True),
        lax.all_gather(grad_rows, ("seq", "rep"), axis=0, tiled=True),
    )
    key_rows = jnp.dot(tokens, w_key, preferred_element_type=jnp.float32).astype(jnp.bfloat16)
    value_rows = jnp.dot(tokens, w_value, preferred_element_type=jnp.float32).astype(jnp.bfloat16)
    live_mask = jnp.arange(tokens.shape[0], dtype=jnp.int32) < counts[0]
    query_heads = head_major(queries, heads_here)
    grad_heads = head_major(grad_att, heads_here)
    key_heads = head_major(key_rows, heads_here)
    value_heads = head_major(value_rows, heads_here)

    def masked_scores(query_head, key_head):
        scores = contract_last(query_head, key_head) * scale
        return jnp.where(live_mask[None, :], scores, -jnp.inf)

    def forward_head(operands):
        query_head, key_head, value_head = operands
        scores = masked_scores(query_head, key_head)
        highest = jnp.max(scores, axis=1)
        expo = jnp.exp(scores - highest[:, None])
        weighted = jnp.dot(
            expo.astype(jnp.bfloat16), value_head, preferred_element_type=jnp.float32
        )
        return (highest, jnp.sum(expo, axis=1), weighted)

    highs, sums, accums = lax.map(forward_head, (query_heads, key_heads, value_heads))
    highs = highs.T
    sums = sums.T
    accums = row_major(accums)
    highest, denominator, numerator = combined_all(
        (highs, sums, accums), ("seq", "rep"), merge_parts
    )
    attention = (numerator / jnp.repeat(denominator, head_size, axis=1)).astype(jnp.bfloat16)
    log_norms = highest + jnp.log(denominator)
    all_rows = attention.shape[0]
    row_terms = jnp.sum(
        (attention.astype(jnp.float32) * grad_att.astype(jnp.float32)).reshape(
            all_rows, heads_here, head_size
        ),
        axis=2,
    )
    attended_rows = lax.dynamic_slice_in_dim(attention, row_start, lat_rows, 0)
    out_terms = jnp.dot(attended_rows, w_out, preferred_element_type=jnp.float32)
    attended = lax.psum_scatter(
        out_terms.astype(jnp.bfloat16), "head", scatter_dimension=1, tiled=True
    )

    def backward_head(operands):
        query_head, key_head, value_head, grad_head, log_norm, row_term = operands
        scores = masked_scores(query_head, key_head)
        weights = jnp.exp(scores - log_norm[:, None])
        grad_value = contract_first(weights.astype(jnp.bfloat16), grad_head).astype(jnp.bfloat16)
        grad_weights = contract_last(grad_head, value_head)
        grad_scores = (weights * (grad_weights - row_term[:, None]) * scale).astype(jnp.bfloat16)
        query_term = jnp.dot(grad_scores, key_head, preferred_element_type=jnp.float32)
        grad_key = contract_first(grad_scores, query_head).astype(jnp.bfloat16)
        return (query_term, grad_key, grad_value)

    query_terms, grad_keys, grad_values = lax.map(
        backward_head, (query_heads, key_heads, value_heads, grad_heads, log_norms.T, row_terms.T)
    )
    query_terms = row_major(query_terms)
    query_total = lax.psum(query_terms, ("seq", "rep"))
    query_grad = lax.dynamic_slice_in_dim(query_total, row_start, lat_rows, 0)
    latent_terms = contract_last(query_grad.astype(jnp.bfloat16), w_query)
    latent_grad = lax.psum_scatter(latent_terms, "head", scatter_dimension=1, tiled=True).astype(
        jnp.bfloat16
    )
    token_terms = contract_last(row_major(grad_keys), w_key) + contract_last(
        row_major(grad_values), w_value
    )
    token_grad = lax.psum_scatter(
        token_terms.astype(jnp.bfloat16), "head", scatter_dimension=1, tiled=True
    )
    return (attended, latent_grad, token_grad)


MESH = pl.DeviceIdType.MESH
BF = jnp.bfloat16
F32 = jnp.float32


def remote(src, dst, send, recv, device):
    return pltpu.make_async_remote_copy(
        src_ref=src, dst_ref=dst, send_sem=send, recv_sem=recv, device_id=device, device_id_type=MESH
    )


def fused_kernel(
    n_seq, n_head, n_rep,
    latents_in, cotangent_in, tokens_in, counts, w_query_in, w_key_in, w_value_in, w_out_in,
    attended, latent_grad, token_grad,
    latents, cotangent, tokens, w_query, w_key, w_value, w_out, in_sem,
    q_all, g_all, g_t, k_all, v_all, k_t, v_t, bias, expo, highs,
    acc_send, acc_recv, st_send, st_recv, norm_row, dq_send, dq_recv, dk, dv, dkv_send, dkv_recv,
    att_stage, att_recv, lat_stage, lat_recv, tok_stage, tok_recv,
    z_send, z_recv, r_send, r_recv, h_send, h_recv,
):
    lat, tok, cols = latents.shape[0], tokens.shape[0], w_query.shape[1]
    hd = D // HEADS
    wide = 2 * hd
    pairs = cols // wide
    scale = hd ** (-0.5)
    z, h, r = lax.axis_index("seq"), lax.axis_index("head"), lax.axis_index("rep")
    other = 1 - r

    def zp(k):
        return lax.rem(z + k, n_seq)

    def hp(k):
        return lax.rem(h + k, n_head)

    loads = [
        pltpu.make_async_copy(source, landing, in_sem.at[i])
        for i, (source, landing) in enumerate((
            (latents_in, latents), (w_query_in, w_query), (tokens_in, tokens), (w_key_in, w_key),
            (w_value_in, w_value), (cotangent_in, cotangent), (w_out_in, w_out),
        ))
    ]
    for load in loads:
        load.start()
    barrier = pltpu.get_barrier_semaphore()
    for k in range(1, n_seq):
        pl.semaphore_signal(barrier, inc=1, device_id={"seq": zp(k)}, device_id_type=MESH)
    for k in range(1, n_head):
        pl.semaphore_signal(barrier, inc=1, device_id={"head": hp(k)}, device_id_type=MESH)
    pl.semaphore_signal(barrier, inc=1, device_id={"rep": other}, device_id_type=MESH)

    def z_copy(kind, src, dst, peer, slot_send, slot_recv):
        return remote(src, dst, z_send.at[kind, slot_send], z_recv.at[kind, slot_recv], {"seq": peer})

    to_right, to_left = z + 1 < n_seq, z > 0

    def line(kind, blocks):
        def copy(owner, peer, slot):
            return z_copy(kind, blocks.at[owner], blocks.at[owner], peer, slot, owner)

        return copy

    q_line, g_line = line(0, q_all), line(1, g_all)

    def visit(k):
        short = jnp.minimum(z, n_seq - 1 - z)
        paired = k <= 2 * short
        far = jnp.where(paired, (k + 1) // 2, k - short)
        from_left = jnp.where(paired, lax.rem(k, 2), jnp.where(z > n_seq - 1 - z, 1, 0)) == 1
        return jnp.where(from_left, z - far, z + far), from_left

    def send_own(copy):
        @pl.when(to_right)
        def _():
            copy(z, z + 1, z).start()

        @pl.when(to_left)
        def _():
            copy(z, z - 1, n_seq).start()

    def own_sent(copy):
        @pl.when(to_right)
        def _():
            copy(z, z + 1, z).wait_send()

        @pl.when(to_left)
        def _():
            copy(z, z - 1, n_seq).wait_send()

    def pass_on(copy, j, from_left):
        copy(j, j, j).wait_recv()

        @pl.when(jnp.logical_and(from_left, to_right))
        def _():
            copy(j, z + 1, j).start()

        @pl.when(jnp.logical_and(jnp.logical_not(from_left), to_left))
        def _():
            copy(j, z - 1, j).start()

    def passed(copy, j, from_left):
        @pl.when(jnp.logical_and(from_left, to_right))
        def _():
            copy(j, z + 1, j).wait_send()

        @pl.when(jnp.logical_and(jnp.logical_not(from_left), to_left))
        def _():
            copy(j, z - 1, j).wait_send()

    def acc_copy(peer, sender):
        return z_copy(2, acc_send.at[peer], acc_recv.at[sender], peer, peer, sender)

    def st_copy(peer, sender):
        return z_copy(3, st_send.at[peer], st_recv.at[sender], peer, peer, sender)

    def norm_copy(peer, owner):
        return z_copy(4, norm_row.at[owner], norm_row.at[owner], peer, peer, owner)

    def dq_copy(peer, sender):
        return z_copy(5, dq_send.at[peer], dq_recv.at[sender], peer, peer, sender)

    def r_copy(index, src, dst):
        return remote(src, dst, r_send.at[index], r_recv.at[index], {"rep": other})

    own, theirs = pl.ds(0, tok), pl.ds(tok, tok)
    k_copy = r_copy(0, k_all.at[own], k_all.at[theirs])
    v_copy = r_copy(1, v_all.at[own], v_all.at[theirs])
    b_copy = r_copy(2, bias.at[own], bias.at[theirs])
    dkv_copy = r_copy(3, dkv_send, dkv_recv)

    def h_copy(index, stage, landing, peer, sender):
        return remote(
            stage.at[peer], landing.at[sender], h_send.at[index, peer], h_recv.at[index, sender], {"head": peer}
        )

    loads[0].wait()
    loads[1].wait()
    q_all[z] = (jnp.dot(latents[...], w_query[...], preferred_element_type=F32).astype(BF) * scale).astype(BF)
    pl.semaphore_wait(barrier, n_seq - 1 + n_head - 1 + 1)
    send_own(q_line)
    loads[2].wait()
    loads[3].wait()
    k_all[own, :] = jnp.dot(tokens[...], w_key[...], preferred_element_type=F32).astype(BF)
    k_copy.start()
    rows = lax.broadcasted_iota(jnp.int32, (tok, 128), 0)
    bias[own, :] = jnp.where(rows < counts[0], 0.0, -jnp.inf).astype(F32)
    b_copy.start()
    loads[4].wait()
    v_all[own, :] = jnp.dot(tokens[...], w_value[...], preferred_element_type=F32).astype(BF)
    v_copy.start()
    loads[5].wait()
    loads[6].wait()
    grads = contract_last(cotangent[...], w_out[...])
    g_all[z] = grads.astype(BF)
    send_own(g_line)
    g_t[...] = grads.T.astype(BF)
    k_t[:, 0:tok] = k_all[own, :].astype(F32).T.astype(BF)
    v_t[:, 0:tok] = v_all[own, :].astype(F32).T.astype(BF)
    k_copy.wait_recv()
    k_t[:, tok:2 * tok] = k_all[theirs, :].astype(F32).T.astype(BF)
    b_copy.wait_recv()
    v_copy.wait_recv()
    v_t[:, tok:2 * tok] = v_all[theirs, :].astype(F32).T.astype(BF)

    lane = lax.broadcasted_iota(jnp.int32, (lat, wide), 1)
    upper = lax.broadcasted_iota(jnp.int32, (wide, lat), 0)

    def stacked(block):
        zero = jnp.zeros_like(block)
        return jnp.concatenate([jnp.where(lane < hd, block, zero), jnp.where(lane < hd, zero, block)], axis=0)

    def halves(both):
        return jnp.where(upper < hd, both[:, :lat], both[:, lat:])

    def forward(j, acc_out, stat_out):
        for p in range(pairs):
            span = slice(p * wide, (p + 1) * wide)
            qs = stacked(q_all[j, :, span])
            live = bias[...]
            scores = contract_last(k_all[:, span], qs)
            scores = scores + jnp.concatenate([live] * (2 * lat // 128), axis=1)
            high = jnp.max(scores, axis=0, keepdims=True)
            e = jnp.exp(scores - high)
            expo[j, p] = e
            highs[j, p] = high
            stat_out[p, 0:1, :] = high
            stat_out[p, 1:2, :] = jnp.sum(e, axis=0, keepdims=True)
            out = jnp.dot(v_t[span, :], e.astype(BF), preferred_element_type=F32)
            acc_out[span, :] = halves(out).astype(BF)

    forward(z, acc_recv.at[z], st_recv.at[z])

    def forward_step(k, carry):
        j, from_left = visit(k)
        pass_on(q_line, j, from_left)
        forward(j, acc_send.at[j], st_send.at[j])
        acc_copy(j, z).start()
        st_copy(j, z).start()
        pass_on(g_line, j, from_left)
        return carry

    lax.fori_loop(1, n_seq, forward_step, 0)

    for k in range(1, n_seq):
        acc_copy(zp(k), zp(k)).wait_recv()
        st_copy(zp(k), zp(k)).wait_recv()

    att_rows = []
    for p in range(pairs):
        span = slice(p * wide, (p + 1) * wide)
        highest = st_recv[0, p, 0:1, :]
        for s in range(1, n_seq):
            highest = jnp.maximum(highest, st_recv[s, p, 0:1, :])
        total = jnp.zeros_like(highest)
        numerator = jnp.zeros((wide, lat), F32)
        for s in range(n_seq):
            factor = jnp.exp(st_recv[s, p, 0:1, :] - highest)
            total = total + st_recv[s, p, 1:2, :] * factor
            spread = jnp.where(upper < hd, factor[:, :lat], factor[:, lat:])
            numerator = numerator + acc_recv[s, span, :].astype(F32) * spread
        below = jnp.where(upper < hd, total[:, :lat], total[:, lat:])
        att = (numerator / below).astype(BF).astype(F32)
        att_rows.append(att)
        product = att * g_t[span, :].astype(F32)
        norm_row[z, p, 0:1, :] = highest + jnp.log(total)
        norm_row[z, p, 1:2, :] = jnp.concatenate(
            [jnp.sum(product[:hd], axis=0, keepdims=True), jnp.sum(product[hd:], axis=0, keepdims=True)], axis=1
        )
    for k in range(1, n_seq):
        norm_copy(zp(k), z).start()

    def stage_columns(stage, terms):
        for g in range(n_head):
            stage[g] = terms[:, g * cols:(g + 1) * cols].astype(BF)

    attention = jnp.concatenate([part.T for part in att_rows], axis=1).astype(BF)
    stage_columns(att_stage, jnp.dot(attention, w_out[...], preferred_element_type=F32))
    for k in range(1, n_head):
        h_copy(0, att_stage, att_recv, hp(k), h).start()

    dk[...] = jnp.zeros_like(dk)
    dv[...] = jnp.zeros_like(dv)

    def backward(j, dq_out):
        for p in range(pairs):
            span = slice(p * wide, (p + 1) * wide)
            qs = stacked(q_all[j, :, span])
            gs = stacked(g_all[j, :, span])
            weights = expo[j, p] * jnp.exp(highs[j, p] - norm_row[j, p, 0:1, :])
            dv[:, span] += jnp.dot(weights.astype(BF), gs, preferred_element_type=F32)
            inner = contract_last(v_all[:, span], gs)
            ds = (weights * (inner - norm_row[j, p, 1:2, :])).astype(BF)
            dk[:, span] += jnp.dot(ds, qs, preferred_element_type=F32)
            both = jnp.dot(k_t[span, :], ds, preferred_element_type=F32)
            dq_out[span, :] = (halves(both) * scale).astype(BF)

    backward(z, dq_recv.at[z])

    def backward_step(k, carry):
        j, _ = visit(k)
        norm_copy(j, j).wait_recv()
        backward(j, dq_send.at[j])
        dq_copy(j, z).start()
        return carry

    lax.fori_loop(1, n_seq, backward_step, 0)

    dkv_send[0] = dk[theirs, :].astype(BF)
    dkv_send[1] = dv[theirs, :].astype(BF)
    dkv_copy.start()

    dkv_copy.wait_recv()
    grad_key = (dk[own, :] + dkv_recv[0].astype(F32)).astype(BF)
    grad_value = (dv[own, :] + dkv_recv[1].astype(F32)).astype(BF)
    stage_columns(tok_stage, contract_last(grad_key, w_key[...]) + contract_last(grad_value, w_value[...]))
    for k in range(1, n_head):
        h_copy(1, tok_stage, tok_recv, hp(k), h).start()

    for k in range(1, n_seq):
        dq_copy(zp(k), zp(k)).wait_recv()
    total_t = dq_recv[0].astype(F32)
    for s in range(1, n_seq):
        total_t = total_t + dq_recv[s].astype(F32)
    stage_columns(lat_stage, contract_last(total_t.T.astype(BF), w_query[...]))
    for k in range(1, n_head):
        h_copy(2, lat_stage, lat_recv, hp(k), h).start()

    def summed(index, stage, landing, out):
        total = stage[h].astype(F32)
        for k in range(1, n_head):
            h_copy(index, stage, landing, hp(k), hp(k)).wait_recv()
            total = total + landing[hp(k)].astype(F32)
        out[...] = total.astype(BF)

    summed(0, att_stage, att_recv, attended)
    summed(1, tok_stage, tok_recv, token_grad)
    summed(2, lat_stage, lat_recv, latent_grad)

    for k in range(1, n_seq):
        peer = zp(k)
        for make in (acc_copy, st_copy, norm_copy, dq_copy):
            make(peer, z).wait_send()

    def drain(k, carry):
        j, from_left = visit(k)
        passed(q_line, j, from_left)
        passed(g_line, j, from_left)
        return carry

    lax.fori_loop(1, n_seq, drain, 0)
    own_sent(q_line)
    own_sent(g_line)
    for copy in (k_copy, v_copy, b_copy, dkv_copy):
        copy.wait_send()
    for k in range(1, n_head):
        h_copy(0, att_stage, att_recv, hp(k), h).wait_send()
        h_copy(1, tok_stage, tok_recv, hp(k), h).wait_send()
        h_copy(2, lat_stage, lat_recv, hp(k), h).wait_send()


def fused(n_seq, n_head, n_rep, latents, cotangent, tokens, counts, w_query, w_key, w_value, w_out):
    lat, tok, cols = latents.shape[0], tokens.shape[0], w_query.shape[1]
    wide = 2 * D // HEADS
    pairs = cols // wide
    vmem = pltpu.VMEM
    dma = pltpu.SemaphoreType.DMA
    stats = vmem((n_seq, pairs, 2, 2 * lat), F32)
    block = vmem((n_seq, cols, lat), BF)
    held = [latents, cotangent, tokens, w_query, w_key, w_value, w_out]
    scratch = [vmem(array.shape, array.dtype) for array in held] + [
        dma((7,)),
        vmem((n_seq, lat, cols), BF),
        vmem((n_seq, lat, cols), BF),
        vmem((cols, lat), BF),
        vmem((2 * tok, cols), BF),
        vmem((2 * tok, cols), BF),
        vmem((cols, 2 * tok), BF),
        vmem((cols, 2 * tok), BF),
        vmem((2 * tok, 128), F32),
        vmem((n_seq, pairs, 2 * tok, 2 * lat), F32),
        vmem((n_seq, pairs, 1, 2 * lat), F32),
        block,
        block,
        stats,
        stats,
        stats,
        block,
        block,
        vmem((2 * tok, cols), F32),
        vmem((2 * tok, cols), F32),
        vmem((2, tok, cols), BF),
        vmem((2, tok, cols), BF),
        vmem((n_head, lat, cols), BF),
        vmem((n_head, lat, cols), BF),
        vmem((n_head, lat, cols), BF),
        vmem((n_head, lat, cols), BF),
        vmem((n_head, tok, cols), BF),
        vmem((n_head, tok, cols), BF),
        dma((6, n_seq + 1)),
        dma((6, n_seq)),
        dma((4,)),
        dma((4,)),
        dma((3, n_head)),
        dma((3, n_head)),
    ]
    whole = pl.BlockSpec(memory_space=pltpu.VMEM)
    far = pl.BlockSpec(memory_space=pl.ANY)
    return pl.pallas_call(
        functools.partial(fused_kernel, n_seq, n_head, n_rep),
        out_shape=(
            jax.ShapeDtypeStruct((lat, cols), BF),
            jax.ShapeDtypeStruct((lat, cols), BF),
            jax.ShapeDtypeStruct((tok, cols), BF),
        ),
        in_specs=[far] * 3 + [pl.BlockSpec(memory_space=pltpu.SMEM)] + [far] * 4,
        out_specs=(whole,) * 3,
        scratch_shapes=scratch,
        compiler_params=pltpu.CompilerParams(
            collective_id=0, has_side_effects=True, vmem_limit_bytes=56 * 1024 * 1024
        ),
    )(latents, cotangent, tokens, counts, w_query, w_key, w_value, w_out)


def solution(mesh):
    in_specs = (
        P(("grp", "seq", "rep"), None),
        P(("grp", "seq", "rep"), None),
        P(("grp", "seq", "rep"), None),
        P(("grp", "seq", "rep")),
        P(None, "head"),
        P(None, "head"),
        P(None, "head"),
        P("head", None),
    )
    out_specs = (
        P(("grp", "seq", "rep"), "head"),
        P(("grp", "seq", "rep"), "head"),
        P(("grp", "seq", "rep"), "head"),
    )
    n_seq, n_head, n_rep = mesh.shape["seq"], mesh.shape["head"], mesh.shape["rep"]

    def body(*operands):
        if operands[0].shape[0] % 128 == 0 and n_rep == 2:
            return fused(n_seq, n_head, n_rep, *operands)
        return on_device(*operands)

    return jax.shard_map(
        body, mesh=mesh, in_specs=in_specs, out_specs=out_specs, check_vma=False
    )
```
